32 devices in a mesh: replica: 2 (over y), blk: 4 (over z), contract: 4 (over x, core).
Axes of the slice: x: 2, y: 2, z: 4, core: 2. Of those that a mesh axis runs over, the one named last changes fastest.
Arguments:
- tokens: bfloat16 [128, 8192], P(('replica', 'blk'), 'contract'), parts along dimension 0, may hold values from -6 to 6
- gate_weight: bfloat16 [8192, 28672], P('contract', 'blk'), may hold values from -0.0625 to 0.0625
- up_weight: bfloat16 [8192, 28672], P('contract', 'blk'), may hold values from -0.0625 to 0.0625
- down_weight: bfloat16 [28672, 8192], P('blk', 'contract'), may hold values from -0.03125 to 0.03125
Outputs:
- mixed: bfloat16 [128, 8192], P(('replica', 'blk'), 'contract'), parts along dimension 0
The draws below stay inside these ranges and needn't reach their ends.
There are 2 independent parts, one for each index of `replica`. The reference program is written for one: setup_inputs(seed, part) draws one part's arguments, and reference() takes and returns one part's arrays. A program takes and returns all parts, laid end to end along the dimension named above; an argument that names none is the same for every part. Nothing has to cross between parts.
All inputs are finite; a program needn't handle non-finite values.
Results may differ from the reference program's by a relative error of at most 0.0049.
Values may be sent and summed in bfloat16 or wider, within the bound.
No kernel may reach another device: no remote copies, remote signals or barrier semaphores. Data moves between devices by JAX's collectives and lax.ppermute only.
A program may use at most 192 MiB of HBM per device.

```python
import jax
import jax.numpy as jnp
from jax import lax

D = 8192
FF = 28672
TOKENS = 64


def shard_levels(key, dims, split, low, top_value):
    def one(dim, shards_of):
        draws = jax.random.uniform(jax.random.fold_in(jax.random.fold_in(key, 6), dim), (shards_of,), jnp.float32, low / len(split), top_value / len(split))
        return jnp.repeat(jnp.exp(draws), dims[dim] // shards_of).reshape((-1,) + (1,) * (len(dims) - dim - 1))

    gain = one(*split[0])
    for cut in split[1:]:
        gain = gain * one(*cut)
    return gain


def bell_draw(rng, dims, width, reach, cuts=(), held_as=jnp.bfloat16):
    drawn = width * jax.random.normal(rng, dims, jnp.float32)
    if cuts:
        drawn = drawn * shard_levels(rng, dims, cuts, -0.22, 0.18)
    return jnp.clip(drawn, -reach, reach).astype(held_as)


def setup_inputs(seed: int = 0, part: int = 0) -> dict:
    arg_keys = jax.random.split(jax.random.key(seed), 5)
    part_splits = jax.random.split(jax.random.fold_in(arg_keys[4], part), 5)
    tokens = bell_draw(part_splits[0], (TOKENS, D), 1.0, 6.0, ((0, 4), (1, 4)))
    gate_weight = bell_draw(arg_keys[1], (D, FF), D ** -0.5, 0.0625, ((0, 4), (1, 4)))
    up_weight = bell_draw(arg_keys[2], (D, FF), D ** -0.5, 0.0625, ((0, 4), (1, 4)))
    down_weight = bell_draw(arg_keys[3], (FF, D), FF ** -0.5, 0.03125, ((0, 4), (1, 4)))
    return dict(tokens=tokens, gate_weight=gate_weight, up_weight=up_weight, down_weight=down_weight)


def product(left, right):
    return jnp.dot(left.astype(jnp.float32), right.astype(jnp.float32), precision=lax.Precision.HIGHEST)


def reference(tokens, gate_weight, up_weight, down_weight):
    gate = product(tokens, gate_weight)
    up = product(tokens, up_weight)
    hidden = (jax.nn.silu(gate) * up).astype(jnp.bfloat16)
    return product(hidden, down_weight).astype(jnp.bfloat16)
```

```python
import functools

import jax
import jax.numpy as jnp
from jax import lax
from jax.experimental import pallas as pl
from jax.experimental.pallas import tpu as pltpu
from jax.sharding import PartitionSpec as P

BF16, F32 = jnp.bfloat16, jnp.float32
MIB = 2**20
CHUNKS = 2
VMEM, ANY = pl.BlockSpec(memory_space=pltpu.VMEM), pl.BlockSpec(memory_space=pl.ANY)


def tile_of(width, most):
    return max(t for t in range(128, most + 1, 128) if width % t == 0)


def reverse(value, count):
    out, bit = 0, 1
    while bit < count:
        out = out * 2 + (value // bit) % 2
        bit *= 2
    return out


def swap(x, axis, count, bit):
    return lax.ppermute(x, axis, [(i, i ^ bit) for i in range(count)])


def stream(sources, buffers, sems, tiles, use):
    depth = sems.shape[0]
    ahead = min(depth, tiles)

    def copies(tile, slot):
        return [
            pltpu.make_async_copy(source(tile), buffer.at[slot], sems.at[slot, i])
            for i, (source, buffer) in enumerate(zip(sources, buffers))
        ]

    for tile in range(ahead):
        for copy in copies(tile, tile):
            copy.start()

    def step(tile, carry):
        slot = lax.rem(tile, depth)
        for copy in copies(tile, slot):
            copy.wait()
        use(tile, slot)

        @pl.when(tile + depth < tiles)
        def _():
            for copy in copies(tile + depth, slot):
                copy.start()

        return carry

    lax.fori_loop(0, tiles, step, 0)


def gate_up_kernel(slots, groups, start, n, bn, *refs):
    pieces = refs[:slots]
    gate, up, keep, send, x, gate_buf, up_buf, sems = refs[slots:]
    block, half = pieces[0].shape[0], keep.shape[0]
    me, per = lax.axis_index("contract"), slots // groups
    for s in range(slots):
        place = reverse(s, slots)
        group = reverse(me ^ (place // per), groups)
        row = pl.multiple_of((group * per + place % per) * block, 16)
        x[pl.ds(row, block), :] = pieces[s][...]

    def source(weight):
        return lambda tile: weight.at[:, pl.ds(pl.multiple_of(start + tile * bn, 128), bn)]

    def use(tile, slot):
        for base, buf in ((0, gate_buf), (n, up_buf)):
            part = jnp.dot(x[...], buf[slot], preferred_element_type=F32)
            columns = pl.ds(pl.multiple_of(base + tile * bn, 128), bn)
            keep[:, columns] = part[:half]
            send[:, columns] = part[half:]

    stream([source(gate), source(up)], [gate_buf, up_buf], sems, n // bn, use)


def gate_up(pieces, gate, up, groups, start, n):
    slots, (block, depth) = len(pieces), pieces[0].shape
    rows, bn, ring = slots * block, tile_of(n, 512), 3
    return pl.pallas_call(
        functools.partial(gate_up_kernel, slots, groups, start, n, bn),
        out_shape=[jax.ShapeDtypeStruct((rows // 2, 2 * n), F32)] * 2,
        in_specs=[VMEM] * slots + [ANY, ANY],
        out_specs=[VMEM, VMEM],
        scratch_shapes=[
            pltpu.VMEM((rows, depth), BF16),
            pltpu.VMEM((ring, depth, bn), BF16),
            pltpu.VMEM((ring, depth, bn), BF16),
            pltpu.SemaphoreType.DMA((ring, 2)),
        ],
        compiler_params=pltpu.CompilerParams(vmem_limit_bytes=30 * MIB),
        cost_estimate=pl.CostEstimate(
            flops=4 * rows * depth * n, bytes_accessed=4 * depth * n, transcendentals=0
        ),
        name="gate_up",
    )(*pieces, gate, up)


def down_kernel(groups, start, bn, last, *refs):
    pieces, refs = refs[:groups], refs[groups:]
    down, refs = refs[0], refs[1:]
    total = None
    if start:
        total, refs = refs[0], refs[1:]
    outs, (hidden, buf, sems) = refs[:-3], refs[-3:]
    share, n = pieces[0].shape
    me = lax.axis_index("contract")
    for j in range(groups):
        row = pl.multiple_of((me ^ j) * share, 16)
        hidden[pl.ds(row, share), :] = pieces[j][...]

    def source(tile):
        return down.at[pl.ds(start, n), pl.ds(pl.multiple_of(tile * bn, 128), bn)]

    def use(tile, slot):
        columns = pl.ds(pl.multiple_of(tile * bn, 128), bn)
        part = jnp.dot(hidden[...], buf[slot], preferred_element_type=F32)
        if total is not None:
            part = part + total[:, columns]
        if last:
            half = outs[0].shape[0]
            outs[0][:, columns] = part[:half]
            outs[1][:, columns] = part[half:].astype(outs[1].dtype)
        else:
            outs[0][:, columns] = part

    stream([source], [buf], sems, down.shape[1] // bn, use)


def down_part(pieces, down, total, start, last, sent):
    groups, (share, n), width = len(pieces), pieces[0].shape, down.shape[1]
    rows, bn, ring = groups * share, tile_of(width, 256), 3
    if last:
        out_shape = [
            jax.ShapeDtypeStruct((rows // 2, width), F32),
            jax.ShapeDtypeStruct((rows // 2, width), sent),
        ]
    else:
        out_shape = [jax.ShapeDtypeStruct((rows, width), F32)]
    given = [] if total is None else [total]
    return pl.pallas_call(
        functools.partial(down_kernel, groups, start, bn, last),
        out_shape=out_shape,
        in_specs=[VMEM] * groups + [ANY] + [VMEM] * len(given),
        out_specs=[VMEM] * len(out_shape),
        scratch_shapes=[
            pltpu.VMEM((rows, n), BF16),
            pltpu.VMEM((ring, n, bn), BF16),
            pltpu.SemaphoreType.DMA((ring, 1)),
        ],
        compiler_params=pltpu.CompilerParams(vmem_limit_bytes=30 * MIB),
        cost_estimate=pl.CostEstimate(
            flops=2 * rows * n * width, bytes_accessed=2 * n * width, transcendentals=0
        ),
        name="down",
    )(*pieces, down, *given)


def gather_tokens(tokens, count):
    pieces, bit = {0: tokens}, count // 2
    while bit:
        pieces.update({s | bit: swap(p, "blk", count, bit) for s, p in list(pieces.items())})
        bit //= 2
    return [pieces[s] for s in range(count)]


def hidden_of(keep, send, groups, n):
    got = swap(send, "contract", groups, 1)
    quarter = keep.shape[0] // 2
    own = keep[:quarter] + got[:quarter]
    away = (keep[quarter:] + got[quarter:]).astype(BF16)
    summed = own + swap(away, "contract", groups, 2).astype(F32)
    mine = (jax.nn.silu(summed[:, :n]) * summed[:, n:]).astype(BF16)
    across = swap(mine, "contract", groups, 2)
    return [
        mine,
        swap(mine, "contract", groups, 1),
        across,
        swap(across, "contract", groups, 1),
    ]


def shards(slots, groups, tokens, gate, up, down):
    pieces = gather_tokens(tokens, slots)
    width = gate.shape[1]
    chunks = CHUNKS if width % (CHUNKS * 128) == 0 else 1
    n = width // chunks
    sent = BF16 if slots <= 4 else F32
    parts = [gate_up(pieces, gate, up, groups, k * n, n) for k in range(chunks)]
    hidden = [hidden_of(keep, send, groups, n) for keep, send in parts]
    total = None
    for k in range(chunks):
        out = down_part(hidden[k], down, total, k * n, k == chunks - 1, sent)
        total = out[0]
    keep, send = out
    bit = 1
    while True:
        keep = keep + swap(send, "blk", slots, bit).astype(F32)
        bit *= 2
        if bit == slots:
            return keep.astype(BF16)
        half = keep.shape[0] // 2
        keep, send = keep[:half], keep[half:].astype(sent)


def solution(mesh):
    placed = (
        P(("replica", "blk"), "contract"),
        P("contract", "blk"),
        P("contract", "blk"),
        P("blk", "contract"),
    )
    return jax.shard_map(
        functools.partial(shards, mesh.shape["blk"], mesh.shape["contract"]),
        mesh=mesh,
        in_specs=placed,
        out_specs=P(("replica", "blk"), "contract"),
        check_vma=False,
    )
```

```python
import functools

import jax
import jax.numpy as jnp
from jax import lax
from jax.experimental import pallas as pl
from jax.experimental.pallas import tpu as pltpu
from jax.sharding import PartitionSpec as P

BF16, F32 = jnp.bfloat16, jnp.float32
MIB = 2**20
SPLIT = (4, 4)
VMEM, ANY = pl.BlockSpec(memory_space=pltpu.VMEM), pl.BlockSpec(memory_space=pl.ANY)
LONG = pl.CostEstimate(flops=20_000_000_000, bytes_accessed=1000, transcendentals=0)


def tile_of(width, most):
    return max(t for t in range(128, most + 1, 128) if width % t == 0)


def reverse(value, count):
    out, bit = 0, 1
    while bit < count:
        out = out * 2 + (value // bit) % 2
        bit *= 2
    return out


def swap(x, axis, count, bit):
    return lax.ppermute(x, axis, [(i, i ^ bit) for i in range(count)])


def local(kernel, outs, *given, name, limit=8 * MIB, cost=None):
    arrays = [a[0] if isinstance(a, list) else a for a in given]
    return pl.pallas_call(
        kernel,
        out_shape=[jax.ShapeDtypeStruct(*o) for o in outs],
        in_specs=[ANY if isinstance(a, list) else VMEM for a in given],
        out_specs=[VMEM] * len(outs),
        compiler_params=pltpu.CompilerParams(vmem_limit_bytes=limit),
        cost_estimate=cost,
        name=name,
    )(*arrays)


def head(tokens):
    def kernel(given, out):
        out[...] = given[...]

    return local(kernel, [(tokens.shape, BF16)], tokens, name="head", cost=LONG)[0]


def gate_up_kernel(slots, groups, waits, start, n, bn, *refs):
    pieces, refs = refs[:slots], refs[slots + waits :]
    gate, up, keep, send, x, buffers, sems = refs
    block, half = pieces[0].shape[0], keep.shape[0]
    tiles, ring = n // bn, sems.shape[0]

    def copy(tile):
        columns = pl.ds(start + tile * bn, bn)
        slot = tile % ring
        return pltpu.make_async_copy(up.at[:, columns], buffers.at[slot], sems.at[slot])

    for tile in range(min(ring, tiles)):
        copy(tile).start()
    me, per = lax.axis_index("contract"), slots // groups
    for s in range(slots):
        place = reverse(s, slots)
        group = reverse(me ^ (place // per), groups)
        row = pl.multiple_of((group * per + place % per) * block, 16)
        x[pl.ds(row, block), :] = pieces[s][...]

    def put(column, part):
        keep[:, pl.ds(column, bn)] = part[:half]
        send[:, pl.ds(column, bn)] = part[half:]

    for tile in range(tiles):
        at = tile * bn
        put(at, jnp.dot(x[...], gate[:, pl.ds(start + at, bn)], preferred_element_type=F32))
        copy(tile).wait()
        put(n + at, jnp.dot(x[...], buffers[tile % ring], preferred_element_type=F32))
        if tile + ring < tiles:
            copy(tile + ring).start()


def gate_up(pieces, waits, gate, up, groups, start, n):
    slots, (block, depth) = len(pieces), pieces[0].shape
    rows, bn, ring = slots * block, tile_of(n, 512), 4
    return pl.pallas_call(
        functools.partial(gate_up_kernel, slots, groups, len(waits), start, n, bn),
        out_shape=[jax.ShapeDtypeStruct((rows // 2, 2 * n), F32)] * 2,
        in_specs=[VMEM] * slots + [ANY] * len(waits) + [VMEM, ANY],
        out_specs=[VMEM, VMEM],
        scratch_shapes=[
            pltpu.VMEM((rows, depth), BF16),
            pltpu.VMEM((ring, depth, bn), BF16),
            pltpu.SemaphoreType.DMA((ring,)),
        ],
        compiler_params=pltpu.CompilerParams(vmem_limit_bytes=14 * MIB),
        cost_estimate=pl.CostEstimate(
            flops=4 * rows * depth * n, bytes_accessed=4 * depth * n, transcendentals=0
        ),
        name="gate_up",
    )(*pieces, *waits, gate, up)


def fold(keep, got, cost=None):
    def kernel(keep, got, own, away):
        quarter = own.shape[0]
        own[...] = keep[:quarter] + got[:quarter]
        away[...] = (keep[quarter:] + got[quarter:]).astype(BF16)

    rows, width = keep.shape
    shape = (rows // 2, width)
    return local(kernel, [(shape, F32), (shape, BF16)], keep, got, name="fold", cost=cost)


def activate(own, got):
    def kernel(own, got, out):
        n = out.shape[1]
        gate = own[:, :n] + got[:, :n].astype(F32)
        up = own[:, n:] + got[:, n:].astype(F32)
        out[...] = (jax.nn.silu(gate) * up).astype(BF16)

    rows, width = own.shape
    return local(kernel, [((rows, width // 2), BF16)], own, got, name="activate", cost=LONG)[0]


def down_kernel(chunks, groups, start, bn, places, *refs):
    pieces, refs = refs[: chunks * groups], refs[chunks * groups :]
    down, refs = refs[0], refs[1:]
    total = None
    if start:
        total, refs = refs[0], refs[1:]
    outs, hidden = refs[:-1], refs[-1]
    me, column = lax.axis_index("contract"), 0
    for k in range(chunks):
        share, n = pieces[k * groups].shape
        for j in range(groups):
            row = pl.multiple_of((me ^ j) * share, 16)
            hidden[pl.ds(row, share), pl.ds(column, n)] = pieces[k * groups + j][...]
        column += n
    for column in range(0, down.shape[1], bn):
        columns = pl.ds(column, bn)
        weight = down[pl.ds(start, hidden.shape[1]), columns]
        part = jnp.dot(hidden[...], weight, preferred_element_type=F32)
        if total is not None:
            part = part + total[:, columns]
        for out, (row, count) in zip(outs, places):
            out[:, columns] = part[row : row + count].astype(out.dtype)


def down_part(pieces, down, total, start, places):
    groups, share, n, width = len(pieces[0]), pieces[0][0].shape[0], sum(p[0].shape[1] for p in pieces), down.shape[1]
    rows, bn = groups * share, tile_of(width, 512)
    given = [] if total is None else [total]
    return pl.pallas_call(
        functools.partial(down_kernel, len(pieces), groups, start, bn, [p[:2] for p in places]),
        out_shape=[jax.ShapeDtypeStruct((count, width), kind) for _, count, kind in places],
        in_specs=[VMEM] * (groups * len(pieces)) + [VMEM] + [VMEM] * len(given),
        out_specs=[VMEM] * len(places),
        scratch_shapes=[pltpu.VMEM((rows, n), BF16)],
        compiler_params=pltpu.CompilerParams(vmem_limit_bytes=8 * MIB),
        cost_estimate=pl.CostEstimate(
            flops=2 * rows * n * width, bytes_accessed=2 * n * width, transcendentals=0
        ),
        name="down",
    )(*(q for p in pieces for q in p), down, *given)


def gather_tokens(tokens, count):
    pieces, bit = {0: tokens}, count // 2
    while bit:
        pieces.update({s | bit: swap(p, "blk", count, bit) for s, p in list(pieces.items())})
        bit //= 2
    return [pieces[s] for s in range(count)]


def shards(slots, groups, tokens, gate, up, down):
    rows, width = slots * tokens.shape[0], gate.shape[1]
    gate = pltpu.with_memory_space_constraint(gate, pltpu.VMEM)
    up = pltpu.with_memory_space_constraint(up, pltpu.HBM)
    down = pltpu.with_memory_space_constraint(down, pltpu.VMEM)
    pieces = gather_tokens(head(tokens), slots)
    unit = sum(SPLIT) * 128
    sizes = [width // sum(SPLIT) * s for s in SPLIT] if width % unit == 0 else [width]
    starts = [sum(sizes[:k]) for k in range(len(sizes))]
    waits, folded = [], []
    for k, (start, n) in enumerate(zip(starts, sizes)):
        keep, send = gate_up(pieces, waits, gate, up, groups, start, n)
        got = swap(send, "contract", groups, 1)
        folded.append(fold(keep, got))
        waits = [folded[-1][1]]
    if slots <= 4:
        block = tokens.shape[0]
        places = [(reverse(s, slots) * block, block, BF16 if s else F32) for s in range(slots)]
    else:
        places = [(0, rows // 2, F32), (rows // 2, rows // 2, F32)]
    hiddens = []
    for k, (own, away) in enumerate(folded):
        mine = activate(own, swap(away, "contract", groups, 2))
        across = swap(mine, "contract", groups, 2)
        hidden = [mine, swap(mine, "contract", groups, 1), across, swap(across, "contract", groups, 1)]
        hiddens.append(hidden)
    out = down_part(hiddens, down, None, 0, places)
    if slots <= 4:
        return sum((swap(out[s], "blk", slots, s).astype(F32) for s in range(1, slots)), out[0]).astype(BF16)
    keep, send = out
    bit = 1
    while True:
        keep = keep + swap(send, "blk", slots, bit)
        bit *= 2
        if bit == slots:
            return keep.astype(BF16)
        half = keep.shape[0] // 2
        keep, send = keep[:half], keep[half:]


def solution(mesh):
    placed = (
        P(("replica", "blk"), "contract"),
        P("contract", "blk"),
        P("contract", "blk"),
        P("blk", "contract"),
    )
    return jax.shard_map(
        functools.partial(shards, mesh.shape["blk"], mesh.shape["contract"]),
        mesh=mesh,
        in_specs=placed,
        out_specs=P(("replica", "blk"), "contract"),
        check_vma=False,
    )
```

```python
import functools

import jax
import jax.numpy as jnp
from jax import lax
from jax.experimental import pallas as pl
from jax.experimental.pallas import tpu as pltpu
from jax.sharding import PartitionSpec as P

BF16, F32 = jnp.bfloat16, jnp.float32
MIB = 2**20
SPLIT = (8, 6)
VMEM, ANY = pl.BlockSpec(memory_space=pltpu.VMEM), pl.BlockSpec(memory_space=pl.ANY)
LONG = pl.CostEstimate(flops=20_000_000_000, bytes_accessed=1000, transcendentals=0)


def tile_of(width, most):
    return max(t for t in range(128, most + 1, 128) if width % t == 0)


def reverse(value, count):
    out, bit = 0, 1
    while bit < count:
        out = out * 2 + (value // bit) % 2
        bit *= 2
    return out


def swap(x, axis, count, bit):
    return lax.ppermute(x, axis, [(i, i ^ bit) for i in range(count)])


def local(kernel, outs, *given, name, limit=8 * MIB, cost=None):
    arrays = [a[0] if isinstance(a, list) else a for a in given]
    return pl.pallas_call(
        kernel,
        out_shape=[jax.ShapeDtypeStruct(*o) for o in outs],
        in_specs=[ANY if isinstance(a, list) else VMEM for a in given],
        out_specs=[VMEM] * len(outs),
        compiler_params=pltpu.CompilerParams(vmem_limit_bytes=limit),
        cost_estimate=cost,
        name=name,
    )(*arrays)


def head(tokens):
    def kernel(given, out):
        out[...] = given[...]

    return local(kernel, [(tokens.shape, BF16)], tokens, name="head", cost=LONG)[0]


def gate_up_kernel(slots, groups, waits, start, n, bn, *refs):
    pieces, refs = refs[:slots], refs[slots + waits :]
    gate, up, keep, send, x, buffers, sems = refs
    block, half = pieces[0].shape[0], keep.shape[0]
    tiles, ring = n // bn, sems.shape[0]

    def copy(tile):
        columns = pl.ds(start + tile * bn, bn)
        slot = tile % ring
        return pltpu.make_async_copy(up.at[:, columns], buffers.at[slot], sems.at[slot])

    for tile in range(min(ring, tiles)):
        copy(tile).start()
    me, per = lax.axis_index("contract"), slots // groups
    for s in range(slots):
        place = reverse(s, slots)
        group = reverse(me ^ (place // per), groups)
        row = pl.multiple_of((group * per + place % per) * block, 16)
        x[pl.ds(row, block), :] = pieces[s][...]

    def put(column, part):
        keep[:, pl.ds(column, bn)] = part[:half]
        send[:, pl.ds(column, bn)] = part[half:]

    lead = min(2, tiles)
    for step in range(tiles + lead):
        if step < tiles:
            weight = gate[:, pl.ds(start + step * bn, bn)]
            put(step * bn, jnp.dot(x[...], weight, preferred_element_type=F32))
        tile = step - lead
        if tile < 0:
            continue
        copy(tile).wait()
        put(n + tile * bn, jnp.dot(x[...], buffers[tile % ring], preferred_element_type=F32))
        if tile + ring < tiles:
            copy(tile + ring).start()


def gate_up(pieces, waits, gate, up, groups, start, n):
    slots, (block, depth) = len(pieces), pieces[0].shape
    rows, bn, ring = slots * block, tile_of(n, 512), 4
    return pl.pallas_call(
        functools.partial(gate_up_kernel, slots, groups, len(waits), start, n, bn),
        out_shape=[jax.ShapeDtypeStruct((rows // 2, 2 * n), F32)] * 2,
        in_specs=[VMEM] * slots + [ANY] * len(waits) + [VMEM, ANY],
        out_specs=[VMEM, VMEM],
        scratch_shapes=[
            pltpu.VMEM((rows, depth), BF16),
            pltpu.VMEM((ring, depth, bn), BF16),
            pltpu.SemaphoreType.DMA((ring,)),
        ],
        compiler_params=pltpu.CompilerParams(vmem_limit_bytes=14 * MIB),
        cost_estimate=pl.CostEstimate(
            flops=4 * rows * depth * n, bytes_accessed=4 * depth * n, transcendentals=0
        ),
        name="gate_up",
    )(*pieces, *waits, gate, up)


def fold(keep, got, waits, cost=None):
    def kernel(keep, got, *refs):
        own, away = refs[-2:]
        quarter = own.shape[0]
        own[...] = keep[:quarter] + got[:quarter]
        away[...] = (keep[quarter:] + got[quarter:]).astype(BF16)

    rows, width = keep.shape
    shape = (rows // 2, width)
    return local(kernel, [(shape, F32), (shape, BF16)], keep, got, *([w] for w in waits), name="fold", cost=cost)


def activate(own, got):
    def kernel(own, got, out):
        n = out.shape[1]
        gate = own[:, :n] + got[:, :n].astype(F32)
        up = own[:, n:] + got[:, n:].astype(F32)
        out[...] = (jax.nn.silu(gate) * up).astype(BF16)

    rows, width = own.shape
    return local(kernel, [((rows, width // 2), BF16)], own, got, name="activate", cost=LONG)[0]


def down_kernel(chunks, groups, start, bn, places, summed, *refs):
    pieces, refs = refs[: chunks * groups], refs[chunks * groups :]
    down, refs = refs[0], refs[1:]
    total = None
    if summed:
        total, refs = refs[0], refs[1:]
    outs, hidden = refs[:-1], refs[-1]
    me, column = lax.axis_index("contract"), 0
    for k in range(chunks):
        share, n = pieces[k * groups].shape
        for j in range(groups):
            row = pl.multiple_of((me ^ j) * share, 16)
            hidden[pl.ds(row, share), pl.ds(column, n)] = pieces[k * groups + j][...]
        column += n
    for column in range(0, down.shape[1], bn):
        columns = pl.ds(column, bn)
        weight = down[pl.ds(start, hidden.shape[1]), columns]
        part = jnp.dot(hidden[...], weight, preferred_element_type=F32)
        if total is not None:
            part = part + total[:, columns]
        for out, (row, count) in zip(outs, places):
            out[:, columns] = part[row : row + count].astype(out.dtype)


def down_part(pieces, down, total, start, places):
    groups, share, n, width = len(pieces[0]), pieces[0][0].shape[0], sum(p[0].shape[1] for p in pieces), down.shape[1]
    rows, bn = groups * share, tile_of(width, 512)
    given = [] if total is None else [total]
    return pl.pallas_call(
        functools.partial(down_kernel, len(pieces), groups, start, bn, [p[:2] for p in places], bool(given)),
        out_shape=[jax.ShapeDtypeStruct((count, width), kind) for _, count, kind in places],
        in_specs=[VMEM] * (groups * len(pieces)) + [VMEM] + [VMEM] * len(given),
        out_specs=[VMEM] * len(places),
        scratch_shapes=[pltpu.VMEM((rows, n), BF16)],
        compiler_params=pltpu.CompilerParams(vmem_limit_bytes=8 * MIB),
        cost_estimate=pl.CostEstimate(
            flops=2 * rows * n * width, bytes_accessed=2 * n * width, transcendentals=0
        ),
        name="down",
    )(*(q for p in pieces for q in p), down, *given)


def gather_tokens(tokens, count):
    if count <= 4:
        return [tokens] + [swap(tokens, "blk", count, s) for s in range(1, count)]
    pieces, bit = {0: tokens}, count // 2
    while bit:
        pieces.update({s | bit: swap(p, "blk", count, bit) for s, p in list(pieces.items())})
        bit //= 2
    return [pieces[s] for s in range(count)]


def shards(slots, groups, tokens, gate, up, down):
    rows, width = slots * tokens.shape[0], gate.shape[1]
    gate = pltpu.with_memory_space_constraint(gate, pltpu.VMEM)
    up = pltpu.with_memory_space_constraint(up, pltpu.HBM)
    pieces = gather_tokens(head(tokens), slots)
    unit = sum(SPLIT) * 128
    sizes = [width // sum(SPLIT) * s for s in SPLIT] if width % unit == 0 else [width]
    starts = [sum(sizes[:k]) for k in range(len(sizes))]
    waits, mines = [], []
    for k, (start, n) in enumerate(zip(starts, sizes)):
        keep, send = gate_up(pieces, waits, gate, up, groups, start, n)
        got = swap(send, "contract", groups, 1)
        own, away = fold(keep, got, mines[-1:])
        waits = [away]
        mine = activate(own, swap(away, "contract", groups, 2))
        mines.append(mine)
    if slots <= 4:
        block = tokens.shape[0]
        places = [(reverse(s, slots) * block, block, BF16 if s else F32) for s in range(slots)]
    else:
        places = [(0, rows // 2, F32), (rows // 2, rows // 2, F32)]
    hiddens = []
    for mine in mines:
        across = swap(mine, "contract", groups, 2)
        hidden = [mine, swap(mine, "contract", groups, 1), across, swap(across, "contract", groups, 1)]
        hiddens.append(hidden)
    held = pltpu.with_memory_space_constraint(down, pltpu.VMEM)
    out = down_part(hiddens, held, None, 0, places)
    if slots <= 4:
        return sum((swap(out[s], "blk", slots, s).astype(F32) for s in reversed(range(1, slots))), out[0]).astype(BF16)
    keep, send = out
    bit = 1
    while True:
        keep = keep + swap(send, "blk", slots, bit)
        bit *= 2
        if bit == slots:
            return keep.astype(BF16)
        half = keep.shape[0] // 2
        keep, send = keep[:half], keep[half:]


def solution(mesh):
    placed = (
        P(("replica", "blk"), "contract"),
        P("contract", "blk"),
        P("contract", "blk"),
        P("blk", "contract"),
    )
    return jax.shard_map(
        functools.partial(shards, mesh.shape["blk"], mesh.shape["contract"]),
        mesh=mesh,
        in_specs=placed,
        out_specs=P(("replica", "blk"), "contract"),
        check_vma=False,
    )
```

```python
import functools

import jax
import jax.numpy as jnp
from jax import lax
from jax.experimental import pallas as pl
from jax.experimental.pallas import tpu as pltpu
from jax.sharding import PartitionSpec as P

BF16, F32 = jnp.bfloat16, jnp.float32
MIB = 2**20
SPLIT = (8, 6)
VMEM, ANY = pl.BlockSpec(memory_space=pltpu.VMEM), pl.BlockSpec(memory_space=pl.ANY)
LONG = pl.CostEstimate(flops=20_000_000_000, bytes_accessed=1000, transcendentals=0)


def tile_of(width, most):
    return max(t for t in range(128, most + 1, 128) if width % t == 0)


def reverse(value, count):
    out, bit = 0, 1
    while bit < count:
        out = out * 2 + (value // bit) % 2
        bit *= 2
    return out


def swap(x, axis, count, bit):
    return lax.ppermute(x, axis, [(i, i ^ bit) for i in range(count)])


def local(kernel, outs, *given, name, limit=8 * MIB, cost=None):
    arrays = [a[0] if isinstance(a, list) else a for a in given]
    return pl.pallas_call(
        kernel,
        out_shape=[jax.ShapeDtypeStruct(*o) for o in outs],
        in_specs=[ANY if isinstance(a, list) else VMEM for a in given],
        out_specs=[VMEM] * len(outs),
        compiler_params=pltpu.CompilerParams(vmem_limit_bytes=limit),
        cost_estimate=cost,
        name=name,
    )(*arrays)


def head(tokens):
    def kernel(given, out):
        out[...] = given[...]

    return local(kernel, [(tokens.shape, BF16)], tokens, name="head", cost=LONG)[0]


def gate_up_kernel(slots, groups, waits, start, n, bn, *refs):
    pieces, refs = refs[:slots], refs[slots + waits :]
    gate, up, keep, send, x, buffers, sems = refs
    block, half = pieces[0].shape[0], keep.shape[0]
    tiles, ring = n // bn, sems.shape[0]

    def copy(tile):
        columns = pl.ds(start + tile * bn, bn)
        slot = tile % ring
        return pltpu.make_async_copy(up.at[:, columns], buffers.at[slot], sems.at[slot])

    for tile in range(min(ring, tiles)):
        copy(tile).start()
    me, per = lax.axis_index("contract"), slots // groups
    for s in range(slots):
        place = reverse(s, slots)
        group = reverse(me ^ (place // per), groups)
        row = pl.multiple_of((group * per + place % per) * block, 16)
        x[pl.ds(row, block), :] = pieces[s][...]

    def put(column, part):
        keep[:, pl.ds(column, bn)] = part[:half]
        send[:, pl.ds(column, bn)] = part[half:]

    lead = min(3, tiles)
    for step in range(tiles + lead):
        if step < tiles:
            weight = gate[:, pl.ds(start + step * bn, bn)]
            put(step * bn, jnp.dot(x[...], weight, preferred_element_type=F32))
        tile = step - lead
        if tile < 0:
            continue
        copy(tile).wait()
        put(n + tile * bn, jnp.dot(x[...], buffers[tile % ring], preferred_element_type=F32))
        if tile + ring < tiles:
            copy(tile + ring).start()


def gate_up(pieces, waits, gate, up, groups, start, n):
    slots, (block, depth) = len(pieces), pieces[0].shape
    rows, bn, ring = slots * block, tile_of(n, 512), 6
    return pl.pallas_call(
        functools.partial(gate_up_kernel, slots, groups, len(waits), start, n, bn),
        out_shape=[jax.ShapeDtypeStruct((rows // 2, 2 * n), F32)] * 2,
        in_specs=[VMEM] * slots + [ANY] * len(waits) + [VMEM, ANY],
        out_specs=[VMEM, VMEM],
        scratch_shapes=[
            pltpu.VMEM((rows, depth), BF16),
            pltpu.VMEM((ring, depth, bn), BF16),
            pltpu.SemaphoreType.DMA((ring,)),
        ],
        compiler_params=pltpu.CompilerParams(vmem_limit_bytes=18 * MIB),
        cost_estimate=pl.CostEstimate(
            flops=4 * rows * depth * n, bytes_accessed=4 * depth * n, transcendentals=0
        ),
        name="gate_up",
    )(*pieces, *waits, gate, up)


def fold(keep, got, waits, cost=None):
    def kernel(keep, got, *refs):
        own, away = refs[-2:]
        quarter = own.shape[0]
        own[...] = keep[:quarter] + got[:quarter]
        away[...] = (keep[quarter:] + got[quarter:]).astype(BF16)

    rows, width = keep.shape
    shape = (rows // 2, width)
    return local(kernel, [(shape, F32), (shape, BF16)], keep, got, *([w] for w in waits), name="fold", cost=cost)


def activate(own, got):
    def kernel(own, got, out):
        n = out.shape[1]
        gate = own[:, :n] + got[:, :n].astype(F32)
        up = own[:, n:] + got[:, n:].astype(F32)
        out[...] = (jax.nn.silu(gate) * up).astype(BF16)

    rows, width = own.shape
    return local(kernel, [((rows, width // 2), BF16)], own, got, name="activate", cost=LONG)[0]


def down_kernel(chunks, groups, start, bn, places, summed, *refs):
    pieces, refs = refs[: chunks * groups], refs[chunks * groups :]
    down, refs = refs[0], refs[1:]
    total = None
    if summed:
        total, refs = refs[0], refs[1:]
    outs, hidden = refs[:-1], refs[-1]
    me, column = lax.axis_index("contract"), 0
    for k in range(chunks):
        share, n = pieces[k * groups].shape
        for j in range(groups):
            row = pl.multiple_of((me ^ j) * share, 16)
            hidden[pl.ds(row, share), pl.ds(column, n)] = pieces[k * groups + j][...]
        column += n
    for column in range(0, down.shape[1], bn):
        columns = pl.ds(column, bn)
        weight = down[pl.ds(start, hidden.shape[1]), columns]
        part = jnp.dot(hidden[...], weight, preferred_element_type=F32)
        if total is not None:
            part = part + total[:, columns]
        for out, (row, count) in zip(outs, places):
            out[:, columns] = part[row : row + count].astype(out.dtype)


def down_part(pieces, down, total, start, places):
    groups, share, n, width = len(pieces[0]), pieces[0][0].shape[0], sum(p[0].shape[1] for p in pieces), down.shape[1]
    rows, bn = groups * share, tile_of(width, 512)
    given = [] if total is None else [total]
    return pl.pallas_call(
        functools.partial(down_kernel, len(pieces), groups, start, bn, [p[:2] for p in places], bool(given)),
        out_shape=[jax.ShapeDtypeStruct((count, width), kind) for _, count, kind in places],
        in_specs=[VMEM] * (groups * len(pieces)) + [VMEM] + [VMEM] * len(given),
        out_specs=[VMEM] * len(places),
        scratch_shapes=[pltpu.VMEM((rows, n), BF16)],
        compiler_params=pltpu.CompilerParams(vmem_limit_bytes=8 * MIB),
        cost_estimate=pl.CostEstimate(
            flops=2 * rows * n * width, bytes_accessed=2 * n * width, transcendentals=0
        ),
        name="down",
    )(*(q for p in pieces for q in p), down, *given)


def gather_tokens(tokens, count):
    if count <= 4:
        return [tokens] + [swap(tokens, "blk", count, s) for s in range(1, count)]
    pieces, bit = {0: tokens}, count // 2
    while bit:
        pieces.update({s | bit: swap(p, "blk", count, bit) for s, p in list(pieces.items())})
        bit //= 2
    return [pieces[s] for s in range(count)]


def shards(slots, groups, tokens, gate, up, down):
    rows, width = slots * tokens.shape[0], gate.shape[1]
    gate = pltpu.with_memory_space_constraint(gate, pltpu.VMEM)
    up = pltpu.with_memory_space_constraint(up, pltpu.HBM)
    pieces = gather_tokens(head(tokens), slots)
    unit = sum(SPLIT) * 128
    sizes = [width // sum(SPLIT) * s for s in SPLIT] if width % unit == 0 else [width]
    starts = [sum(sizes[:k]) for k in range(len(sizes))]
    waits, mines = [], []
    for k, (start, n) in enumerate(zip(starts, sizes)):
        keep, send = gate_up(pieces, waits, gate, up, groups, start, n)
        got = swap(send, "contract", groups, 1)
        own, away = fold(keep, got, mines[-1:])
        waits = [away]
        mine = activate(own, swap(away, "contract", groups, 2))
        mines.append(mine)
    if slots <= 4:
        block = tokens.shape[0]
        places = [(reverse(s, slots) * block, block, BF16 if s else F32) for s in range(slots)]
    else:
        places = [(0, rows // 2, F32), (rows // 2, rows // 2, F32)]
    hiddens = []
    for mine in mines:
        across = swap(mine, "contract", groups, 2)
        hidden = [mine, swap(mine, "contract", groups, 1), across, swap(across, "contract", groups, 1)]
        hiddens.append(hidden)
    held = pltpu.with_memory_space_constraint(down, pltpu.VMEM)
    out = down_part(hiddens, held, None, 0, places)
    if slots <= 4:
        return sum((swap(out[s], "blk", slots, s).astype(F32) for s in reversed(range(1, slots))), out[0]).astype(BF16)
    keep, send = out
    bit = 1
    while True:
        keep = keep + swap(send, "blk", slots, bit)
        bit *= 2
        if bit == slots:
            return keep.astype(BF16)
        half = keep.shape[0] // 2
        keep, send = keep[:half], keep[half:]


def solution(mesh):
    placed = (
        P(("replica", "blk"), "contract"),
        P("contract", "blk"),
        P("contract", "blk"),
        P("blk", "contract"),
    )
    return jax.shard_map(
        functools.partial(shards, mesh.shape["blk"], mesh.shape["contract"]),
        mesh=mesh,
        in_specs=placed,
        out_specs=P(("replica", "blk"), "contract"),
        check_vma=False,
    )
```

```python
import functools

import jax
import jax.numpy as jnp
from jax import lax
from jax.experimental import pallas as pl
from jax.experimental.pallas import tpu as pltpu
from jax.sharding import PartitionSpec as P

BF16, F32 = jnp.bfloat16, jnp.float32
MIB = 2**20
SPLIT = (8, 1, 5)
VMEM, ANY = pl.BlockSpec(memory_space=pltpu.VMEM), pl.BlockSpec(memory_space=pl.ANY)
LONG = pl.CostEstimate(flops=20_000_000_000, bytes_accessed=1000, transcendentals=0)


def tile_of(width, most):
    return max(t for t in range(128, most + 1, 128) if width % t == 0)


def reverse(value, count):
    out, bit = 0, 1
    while bit < count:
        out = out * 2 + (value // bit) % 2
        bit *= 2
    return out


def swap(x, axis, count, bit):
    return lax.ppermute(x, axis, [(i, i ^ bit) for i in range(count)])


def local(kernel, outs, *given, name, limit=8 * MIB, cost=None):
    arrays = [a[0] if isinstance(a, list) else a for a in given]
    return pl.pallas_call(
        kernel,
        out_shape=[jax.ShapeDtypeStruct(*o) for o in outs],
        in_specs=[ANY if isinstance(a, list) else VMEM for a in given],
        out_specs=[VMEM] * len(outs),
        compiler_params=pltpu.CompilerParams(vmem_limit_bytes=limit),
        cost_estimate=cost,
        name=name,
    )(*arrays)


def head(tokens):
    def kernel(given, out):
        out[...] = given[...]

    return local(kernel, [(tokens.shape, BF16)], tokens, name="head", cost=LONG)[0]


def gate_up_kernel(slots, groups, waits, start, n, bn, *refs):
    pieces, refs = refs[:slots], refs[slots + waits :]
    gate, up, keep, send, x, buffers, sems = refs
    block, half = pieces[0].shape[0], keep.shape[0]
    tiles, ring = n // bn, sems.shape[0]

    def copy(tile):
        columns = pl.ds(start + tile * bn, bn)
        slot = tile % ring
        return pltpu.make_async_copy(up.at[:, columns], buffers.at[slot], sems.at[slot])

    for tile in range(min(ring, tiles)):
        copy(tile).start()
    me, per = lax.axis_index("contract"), slots // groups
    for s in range(slots):
        place = reverse(s, slots)
        group = reverse(me ^ (place // per), groups)
        row = pl.multiple_of((group * per + place % per) * block, 16)
        x[pl.ds(row, block), :] = pieces[s][...]

    def put(column, part):
        keep[:, pl.ds(column, bn)] = part[:half]
        send[:, pl.ds(column, bn)] = part[half:]

    lead = min(3, tiles)
    for step in range(tiles + lead):
        if step < tiles:
            weight = gate[:, pl.ds(start + step * bn, bn)]
            put(step * bn, jnp.dot(x[...], weight, preferred_element_type=F32))
        tile = step - lead
        if tile < 0:
            continue
        copy(tile).wait()
        put(n + tile * bn, jnp.dot(x[...], buffers[tile % ring], preferred_element_type=F32))
        if tile + ring < tiles:
            copy(tile + ring).start()


def gate_up(pieces, waits, gate, up, groups, start, n):
    slots, (block, depth) = len(pieces), pieces[0].shape
    rows, bn, ring = slots * block, tile_of(n, 512), 6
    return pl.pallas_call(
        functools.partial(gate_up_kernel, slots, groups, len(waits), start, n, bn),
        out_shape=[jax.ShapeDtypeStruct((rows // 2, 2 * n), F32)] * 2,
        in_specs=[VMEM] * slots + [ANY] * len(waits) + [VMEM, ANY],
        out_specs=[VMEM, VMEM],
        scratch_shapes=[
            pltpu.VMEM((rows, depth), BF16),
            pltpu.VMEM((ring, depth, bn), BF16),
            pltpu.SemaphoreType.DMA((ring,)),
        ],
        compiler_params=pltpu.CompilerParams(vmem_limit_bytes=18 * MIB),
        cost_estimate=pl.CostEstimate(
            flops=4 * rows * depth * n, bytes_accessed=4 * depth * n, transcendentals=0
        ),
        name="gate_up",
    )(*pieces, *waits, gate, up)


def fold(parts, waits):
    rows, count = parts[0][0].shape[0], len(parts)
    width = sum(keep.shape[1] for keep, _ in parts)

    def kernel(*refs):
        own, away = refs[-2:]
        quarter, at = own.shape[0], 0
        for keep, got in zip(refs[:count], refs[count : 2 * count]):
            n = keep.shape[1] // 2
            for base, column in ((0, at), (n, width // 2 + at)):
                here, there = pl.ds(base, n), pl.ds(column, n)
                own[:, there] = keep[:quarter, here] + got[:quarter, here]
                away[:, there] = (keep[quarter:, here] + got[quarter:, here]).astype(BF16)
            at += n

    shape = (rows // 2, width)
    given = [keep for keep, _ in parts] + [got for _, got in parts]
    return local(kernel, [(shape, F32), (shape, BF16)], *given, *([w] for w in waits), name="fold")


def activate(own, got):
    def kernel(own, got, out):
        n = out.shape[1]
        gate = own[:, :n] + got[:, :n].astype(F32)
        up = own[:, n:] + got[:, n:].astype(F32)
        out[...] = (jax.nn.silu(gate) * up).astype(BF16)

    rows, width = own.shape
    return local(kernel, [((rows, width // 2), BF16)], own, got, name="activate", cost=LONG)[0]


def down_kernel(chunks, groups, start, bn, places, summed, *refs):
    pieces, refs = refs[: chunks * groups], refs[chunks * groups :]
    down, refs = refs[0], refs[1:]
    total = None
    if summed:
        total, refs = refs[0], refs[1:]
    outs, hidden = refs[:-1], refs[-1]
    me, column = lax.axis_index("contract"), 0
    for k in range(chunks):
        share, n = pieces[k * groups].shape
        for j in range(groups):
            row = pl.multiple_of((me ^ j) * share, 16)
            hidden[pl.ds(row, share), pl.ds(column, n)] = pieces[k * groups + j][...]
        column += n
    for column in range(0, down.shape[1], bn):
        columns = pl.ds(column, bn)
        weight = down[pl.ds(start, hidden.shape[1]), columns]
        part = jnp.dot(hidden[...], weight, preferred_element_type=F32)
        if total is not None:
            part = part + total[:, columns]
        for out, (row, count) in zip(outs, places):
            out[:, columns] = part[row : row + count].astype(out.dtype)


def down_part(pieces, down, total, start, places):
    groups, share, n, width = len(pieces[0]), pieces[0][0].shape[0], sum(p[0].shape[1] for p in pieces), down.shape[1]
    rows, bn = groups * share, tile_of(width, 512)
    given = [] if total is None else [total]
    return pl.pallas_call(
        functools.partial(down_kernel, len(pieces), groups, start, bn, [p[:2] for p in places], bool(given)),
        out_shape=[jax.ShapeDtypeStruct((count, width), kind) for _, count, kind in places],
        in_specs=[VMEM] * (groups * len(pieces)) + [VMEM] + [VMEM] * len(given),
        out_specs=[VMEM] * len(places),
        scratch_shapes=[pltpu.VMEM((rows, n), BF16)],
        compiler_params=pltpu.CompilerParams(vmem_limit_bytes=8 * MIB),
        cost_estimate=pl.CostEstimate(
            flops=2 * rows * n * width, bytes_accessed=2 * n * width, transcendentals=0
        ),
        name="down",
    )(*(q for p in pieces for q in p), down, *given)


def take(x):
    def kernel(given, out):
        out[...] = given[...]

    return local(kernel, [(x.shape, x.dtype)], x, name="take", limit=MIB)[0]


def plus(total, got):
    def kernel(total, got, out):
        out[...] = total[...] + got[...].astype(F32)

    return local(kernel, [(total.shape, F32)], total, got, name="plus", limit=2 * MIB)[0]


def gather_tokens(tokens, count):
    if count <= 4:
        pieces = [tokens] + [swap(tokens, "blk", count, s) for s in range(1, count)]
        return pieces[:-1] + [take(pieces[-1])]
    pieces, bit = {0: tokens}, count // 2
    while bit:
        pieces.update({s | bit: swap(p, "blk", count, bit) for s, p in list(pieces.items())})
        bit //= 2
    return [pieces[s] for s in range(count)]


def shards(slots, groups, tokens, gate, up, down):
    rows, width = slots * tokens.shape[0], gate.shape[1]
    gate = pltpu.with_memory_space_constraint(gate, pltpu.VMEM)
    up = pltpu.with_memory_space_constraint(up, pltpu.HBM)
    pieces = gather_tokens(head(tokens), slots)
    unit = width // sum(SPLIT) if width % (sum(SPLIT) * 128) == 0 else 0
    sizes = [unit * n for n in SPLIT] if unit else [width]

    def products(k, waits):
        keep, send = gate_up(pieces, waits, gate, up, groups, sum(sizes[:k]), sizes[k])
        return keep, swap(send, "contract", groups, 1)

    def across_sum(own, away):
        return activate(own, swap(away, "contract", groups, 2))

    first = products(0, [])
    if unit:
        second = products(1, first[:1])
        own, away = fold([first], second[:1])
        mines = [across_sum(own, away)]
        third = products(2, [away])
        mines.append(across_sum(*fold([second, third], mines)))
    else:
        mines = [across_sum(*fold([first], []))]
    if slots <= 4:
        block = tokens.shape[0]
        places = [(reverse(s, slots) * block, block, BF16 if s else F32) for s in range(slots)]
    else:
        places = [(0, rows // 2, F32), (rows // 2, rows // 2, F32)]
    hiddens = []
    for mine in mines:
        across = swap(mine, "contract", groups, 2)
        hidden = [mine, swap(mine, "contract", groups, 1), across, swap(across, "contract", groups, 1)]
        hiddens.append(hidden)
    held = pltpu.with_memory_space_constraint(down, pltpu.VMEM)
    out = down_part(hiddens, held, None, 0, places)
    if slots <= 4:
        got = [swap(out[s], "blk", slots, s) for s in range(1, slots)]
        total = plus(out[0], got.pop())
        return sum((g.astype(F32) for g in reversed(got)), total).astype(BF16)
    keep, send = out
    bit = 1
    while True:
        keep = keep + swap(send, "blk", slots, bit)
        bit *= 2
        if bit == slots:
            return keep.astype(BF16)
        half = keep.shape[0] // 2
        keep, send = keep[:half], keep[half:]


def solution(mesh):
    placed = (
        P(("replica", "blk"), "contract"),
        P("contract", "blk"),
        P("contract", "blk"),
        P("blk", "contract"),
    )
    return jax.shard_map(
        functools.partial(shards, mesh.shape["blk"], mesh.shape["contract"]),
        mesh=mesh,
        in_specs=placed,
        out_specs=P(("replica", "blk"), "contract"),
        check_vma=False,
    )
```

```python
import functools

import jax
import jax.numpy as jnp
from jax import lax
from jax.experimental import pallas as pl
from jax.experimental.pallas import tpu as pltpu
from jax.sharding import PartitionSpec as P

BF16, F32 = jnp.bfloat16, jnp.float32
MIB = 2**20
SPLIT = (8, 1, 5)
VMEM, ANY = pl.BlockSpec(memory_space=pltpu.VMEM), pl.BlockSpec(memory_space=pl.ANY)
LONG = pl.CostEstimate(flops=20_000_000_000, bytes_accessed=1000, transcendentals=0)


def tile_of(width, most):
    return max(t for t in range(128, most + 1, 128) if width % t == 0)


def reverse(value, count):
    out, bit = 0, 1
    while bit < count:
        out = out * 2 + (value // bit) % 2
        bit *= 2
    return out


def swap(x, axis, count, bit):
    return lax.ppermute(x, axis, [(i, i ^ bit) for i in range(count)])


def local(kernel, outs, *given, name, limit=8 * MIB, cost=None):
    arrays = [a[0] if isinstance(a, list) else a for a in given]
    return pl.pallas_call(
        kernel,
        out_shape=[jax.ShapeDtypeStruct(*o) for o in outs],
        in_specs=[ANY if isinstance(a, list) else VMEM for a in given],
        out_specs=[VMEM] * len(outs),
        compiler_params=pltpu.CompilerParams(vmem_limit_bytes=limit),
        cost_estimate=cost,
        name=name,
    )(*arrays)


def head(tokens):
    def kernel(given, out):
        out[...] = given[...]

    return local(kernel, [(tokens.shape, BF16)], tokens, name="head", cost=LONG)[0]


def gate_up_kernel(slots, groups, waits, start, n, bn, *refs):
    pieces, refs = refs[:slots], refs[slots + waits :]
    gate, up, keep, send, x, buffers, sems = refs
    block, half = pieces[0].shape[0], keep.shape[0]
    tiles, ring = n // bn, sems.shape[0]

    def copy(tile):
        columns = pl.ds(start + tile * bn, bn)
        slot = tile % ring
        return pltpu.make_async_copy(up.at[:, columns], buffers.at[slot], sems.at[slot])

    for tile in range(min(ring, tiles)):
        copy(tile).start()
    me, per = lax.axis_index("contract"), slots // groups
    for s in range(slots):
        place = reverse(s, slots)
        group = reverse(me ^ (place // per), groups)
        row = pl.multiple_of((group * per + place % per) * block, 16)
        x[pl.ds(row, block), :] = pieces[s][...]

    def put(column, part):
        keep[:, pl.ds(column, bn)] = part[:half]
        send[:, pl.ds(column, bn)] = part[half:]

    lead = min(4, tiles)
    for step in range(tiles + lead):
        if step < tiles:
            weight = gate[:, pl.ds(start + step * bn, bn)]
            put(step * bn, jnp.dot(x[...], weight, preferred_element_type=F32))
        tile = step - lead
        if tile < 0:
            continue
        copy(tile).wait()
        put(n + tile * bn, jnp.dot(x[...], buffers[tile % ring], preferred_element_type=F32))
        if tile + ring < tiles:
            copy(tile + ring).start()


def gate_up(pieces, waits, gate, up, groups, start, n):
    slots, (block, depth) = len(pieces), pieces[0].shape
    rows, bn, ring = slots * block, tile_of(n, 512), 8
    return pl.pallas_call(
        functools.partial(gate_up_kernel, slots, groups, len(waits), start, n, bn),
        out_shape=[jax.ShapeDtypeStruct((rows // 2, 2 * n), F32)] * 2,
        in_specs=[VMEM] * slots + [ANY] * len(waits) + [VMEM, ANY],
        out_specs=[VMEM, VMEM],
        scratch_shapes=[
            pltpu.VMEM((rows, depth), BF16),
            pltpu.VMEM((ring, depth, bn), BF16),
            pltpu.SemaphoreType.DMA((ring,)),
        ],
        compiler_params=pltpu.CompilerParams(vmem_limit_bytes=22 * MIB),
        cost_estimate=pl.CostEstimate(
            flops=4 * rows * depth * n, bytes_accessed=4 * depth * n, transcendentals=0
        ),
        name="gate_up",
    )(*pieces, *waits, gate, up)


def fold(parts, waits):
    rows, count = parts[0][0].shape[0], len(parts)
    width = sum(keep.shape[1] for keep, _ in parts)

    def kernel(*refs):
        own, away = refs[-2:]
        quarter, at = own.shape[0], 0
        for keep, got in zip(refs[:count], refs[count : 2 * count]):
            n = keep.shape[1] // 2
            for base, column in ((0, at), (n, width // 2 + at)):
                here, there = pl.ds(base, n), pl.ds(column, n)
                own[:, there] = keep[:quarter, here] + got[:quarter, here]
                away[:, there] = (keep[quarter:, here] + got[quarter:, here]).astype(BF16)
            at += n

    shape = (rows // 2, width)
    given = [keep for keep, _ in parts] + [got for _, got in parts]
    return local(kernel, [(shape, F32), (shape, BF16)], *given, *([w] for w in waits), name="fold")


def activate(own, got):
    def kernel(own, got, out):
        n = out.shape[1]
        gate = own[:, :n] + got[:, :n].astype(F32)
        up = own[:, n:] + got[:, n:].astype(F32)
        out[...] = (jax.nn.silu(gate) * up).astype(BF16)

    rows, width = own.shape
    return local(kernel, [((rows, width // 2), BF16)], own, got, name="activate", cost=LONG)[0]


def down_kernel(chunks, groups, start, bn, places, summed, *refs):
    pieces, refs = refs[: chunks * groups], refs[chunks * groups :]
    down, refs = refs[0], refs[1:]
    total = None
    if summed:
        total, refs = refs[0], refs[1:]
    outs, hidden = refs[:-1], refs[-1]
    me, column = lax.axis_index("contract"), 0
    for k in range(chunks):
        share, n = pieces[k * groups].shape
        for j in range(groups):
            row = pl.multiple_of((me ^ j) * share, 16)
            hidden[pl.ds(row, share), pl.ds(column, n)] = pieces[k * groups + j][...]
        column += n
    for column in range(0, down.shape[1], bn):
        columns = pl.ds(column, bn)
        weight = down[pl.ds(start, hidden.shape[1]), columns]
        part = jnp.dot(hidden[...], weight, preferred_element_type=F32)
        if total is not None:
            part = part + total[:, columns]
        for out, (row, count) in zip(outs, places):
            out[:, columns] = part[row : row + count].astype(out.dtype)


def down_part(pieces, down, total, start, places):
    groups, share, n, width = len(pieces[0]), pieces[0][0].shape[0], sum(p[0].shape[1] for p in pieces), down.shape[1]
    rows, bn = groups * share, tile_of(width, 1024)
    given = [] if total is None else [total]
    return pl.pallas_call(
        functools.partial(down_kernel, len(pieces), groups, start, bn, [p[:2] for p in places], bool(given)),
        out_shape=[jax.ShapeDtypeStruct((count, width), kind) for _, count, kind in places],
        in_specs=[VMEM] * (groups * len(pieces)) + [VMEM] + [VMEM] * len(given),
        out_specs=[VMEM] * len(places),
        scratch_shapes=[pltpu.VMEM((rows, n), BF16)],
        compiler_params=pltpu.CompilerParams(vmem_limit_bytes=8 * MIB),
        cost_estimate=pl.CostEstimate(
            flops=2 * rows * n * width, bytes_accessed=2 * n * width, transcendentals=0
        ),
        name="down",
    )(*(q for p in pieces for q in p), down, *given)


def take(x):
    def kernel(given, out):
        out[...] = given[...]

    return local(kernel, [(x.shape, x.dtype)], x, name="take", limit=MIB)[0]


def plus(total, got):
    def kernel(total, got, out):
        out[...] = total[...] + got[...].astype(F32)

    return local(kernel, [(total.shape, F32)], total, got, name="plus", limit=2 * MIB)[0]


def gather_tokens(tokens, count):
    if count <= 4:
        pieces = [tokens] + [swap(tokens, "blk", count, s) for s in range(1, count)]
        return pieces[:-1] + [take(pieces[-1])]
    pieces, bit = {0: tokens}, count // 2
    while bit:
        pieces.update({s | bit: swap(p, "blk", count, bit) for s, p in list(pieces.items())})
        bit //= 2
    return [pieces[s] for s in range(count)]


def shards(slots, groups, tokens, gate, up, down):
    rows, width = slots * tokens.shape[0], gate.shape[1]
    gate = pltpu.with_memory_space_constraint(gate, pltpu.VMEM)
    up = pltpu.with_memory_space_constraint(up, pltpu.HBM)
    pieces = gather_tokens(head(tokens), slots)
    unit = width // sum(SPLIT) if width % (sum(SPLIT) * 128) == 0 else 0
    sizes = [unit * n for n in SPLIT] if unit else [width]

    def products(k, waits):
        keep, send = gate_up(pieces, waits, gate, up, groups, sum(sizes[:k]), sizes[k])
        return keep, swap(send, "contract", groups, 1)

    def across_sum(own, away):
        return activate(own, swap(away, "contract", groups, 2))

    first = products(0, [])
    if unit:
        second = products(1, first[:1])
        own, away = fold([first], second[:1])
        mines = [across_sum(own, away)]
        third = products(2, [away])
        mines.append(across_sum(*fold([second, third], mines)))
    else:
        mines = [across_sum(*fold([first], []))]
    if slots <= 4:
        block = tokens.shape[0]
        places = [(reverse(s, slots) * block, block, BF16 if s else F32) for s in range(slots)]
    else:
        places = [(0, rows // 2, F32), (rows // 2, rows // 2, F32)]
    hiddens = []
    for mine in mines:
        across = swap(mine, "contract", groups, 2)
        hidden = [mine, swap(mine, "contract", groups, 1), across, swap(across, "contract", groups, 1)]
        hiddens.append(hidden)
    held = pltpu.with_memory_space_constraint(down, pltpu.VMEM)
    out = down_part(hiddens, held, None, 0, places)
    if slots <= 4:
        got = [swap(out[s], "blk", slots, s) for s in range(1, slots)]
        total = plus(out[0], got.pop())
        return sum((g.astype(F32) for g in reversed(got)), total).astype(BF16)
    keep, send = out
    bit = 1
    while True:
        keep = keep + swap(send, "blk", slots, bit)
        bit *= 2
        if bit == slots:
            return keep.astype(BF16)
        half = keep.shape[0] // 2
        keep, send = keep[:half], keep[half:]


def solution(mesh):
    placed = (
        P(("replica", "blk"), "contract"),
        P("contract", "blk"),
        P("contract", "blk"),
        P("blk", "contract"),
    )
    return jax.shard_map(
        functools.partial(shards, mesh.shape["blk"], mesh.shape["contract"]),
        mesh=mesh,
        in_specs=placed,
        out_specs=P(("replica", "blk"), "contract"),
        check_vma=False,
    )
```
